32 devices in a mesh: rep: 8 (over z, x), shard: 4 (over y, core).
Axes of the slice: x: 2, y: 2, z: 4, core: 2. Of those that a mesh axis runs over, the one named last changes fastest.
Arguments:
- tokens: bfloat16 [16384, 768], P(('rep', 'shard')), may hold values from -6 to 6
- cotangent: bfloat16 [16384, 768], P(('rep', 'shard')), may hold values from -6 to 6
- segment: int32 [16384], replicated, may hold values from 0 to 11, as said below
- w_qkv: bfloat16 [768, 2304], P('shard'), may hold values from -0.21875 to 0.21875
- bias_query: bfloat16 [768], P('shard'), may hold values from -1.5 to 1.5
- bias_value: bfloat16 [768], P('shard'), may hold values from -1.5 to 1.5
- w_out: bfloat16 [768, 768], P('shard'), may hold values from -6 to 6
- bias_out: bfloat16 [768], P('shard'), may hold values from -1.5 to 1.5
- ln1_gain: bfloat16 [768], P('shard'), may hold values from 0.5 to 1.5
- ln1_bias: bfloat16 [768], P('shard'), may hold values from -1.5 to 1.5
- ln2_gain: bfloat16 [768], P('shard'), may hold values from 0.5 to 1.5
- ln2_bias: bfloat16 [768], P('shard'), may hold values from -1.5 to 1.5
- w_up: bfloat16 [768, 3072], P('shard'), may hold values from -0.21875 to 0.21875
- bias_up: bfloat16 [3072], P('shard'), may hold values from -1.5 to 1.5
- w_down: bfloat16 [3072, 768], P('shard'), may hold values from -0.109375 to 0.109375
- bias_down: bfloat16 [768], P('shard'), may hold values from -1.5 to 1.5
Outputs:
- layer_out: float32 [16384, 768], P(('rep', 'shard'))
- grad_input: float32 [16384, 768], P(('rep', 'shard'))
- grad_w_qkv: float32 [768, 2304], P('shard')
- grad_bias_query: float32 [768], P('shard')
- grad_bias_value: float32 [768], P('shard')
- grad_w_out: float32 [768, 768], P('shard')
- grad_bias_out: float32 [768], P('shard')
- grad_ln1_gain: float32 [768], P('shard')
- grad_ln1_bias: float32 [768], P('shard')
- grad_ln2_gain: float32 [768], P('shard')
- grad_ln2_bias: float32 [768], P('shard')
- grad_w_up: float32 [768, 3072], P('shard')
- grad_bias_up: float32 [3072], P('shard')
- grad_w_down: float32 [3072, 768], P('shard')
- grad_bias_down: float32 [768], P('shard')
The draws below stay inside these ranges and needn't reach their ends.
Inputs may be any that keep to these rules, and one draw needn't show every extreme that they name: `segment`: never falls along the stream and starts at 0; each run of one value is one sequence of 1024 to 2048 tokens, one run holds exactly 2048; every aligned stretch of 4096 tokens holds exactly three whole sequences.
All inputs are finite; a program needn't handle non-finite values.
Results may differ from the reference program's by a relative error of at most 0.013.
Values may be sent and summed in bfloat16 or wider, within the bound.
A program may use at most 320 MiB of HBM per device.

```python
import jax
import jax.numpy as jnp
from jax import lax

D = 768
H = 12
HD = 64
FF = 3072
TOK_DEV = 512
LOOK = 4
SEG_MOST = 2048
TOKENS = 16384


def draw_segment(key, part):
    key = jax.random.fold_in(key, 11)
    units = TOKENS // (2 * SEG_MOST)
    half = SEG_MOST // 2
    first_key, second_key = jax.random.split(key)
    first_len = jax.random.randint(first_key, (units,), half, SEG_MOST + 1)
    first_len = jnp.where(jnp.arange(units) == 0, SEG_MOST, first_len).astype(jnp.int32)
    second_len = jax.random.randint(second_key, (units,), half, 3 * half - first_len + 1).astype(jnp.int32)
    third_len = 2 * SEG_MOST - first_len - second_len
    lengths = jnp.stack([first_len, second_len, third_len], axis=1).reshape(3 * units)
    ends = jnp.cumsum(lengths)
    places = jnp.arange(TOKENS, dtype=jnp.int32)
    return jnp.sum((ends[None, :] <= places[:, None]).astype(jnp.int32), axis=1).astype(jnp.int32)


def shard_levels(rng, shape, cuts, low, high):
    level = 1.0
    for position, blocks in cuts:
        draws = jax.random.uniform(jax.random.fold_in(jax.random.fold_in(rng, 6), position), (blocks,), jnp.float32, low / len(cuts), high / len(cuts))
        level = level * jnp.repeat(jnp.exp(draws), shape[position] // blocks).reshape((-1,) + (1,) * (len(shape) - 1 - position))
    return level


def normal_values(rng, extent, scale, most, cuts=(), kind=jnp.bfloat16):
    entries = scale * jax.random.normal(rng, extent, jnp.float32)
    if cuts:
        entries = entries * shard_levels(rng, extent, cuts, -0.22, 0.18)
    return jnp.clip(entries, -most, most).astype(kind)


def setup_inputs(seed: int = 0) -> dict:
    splits = jax.random.split(jax.random.key(seed), 17)
    tokens = normal_values(splits[0], (TOKENS, D), 1.0, 6.0, ((0, 32),))
    cotangent = normal_values(splits[1], (TOKENS, D), 1.0, 6.0, ((0, 32),))
    segment = draw_segment(jax.random.fold_in(splits[16], 71), 0)
    w_qkv = normal_values(splits[3], (D, 3 * D), D ** -0.5, 0.21875, ((0, 4),))
    bias_query = normal_values(splits[4], (D,), 0.3, 1.5, ((0, 4),))
    bias_value = normal_values(splits[5], (D,), 0.3, 1.5, ((0, 4),))
    w_out = normal_values(splits[6], (D, D), ((SEG_MOST // 2) ** 0.5 * D ** -0.5), 6.0, ((0, 4),))
    bias_out = normal_values(splits[7], (D,), 0.3, 1.5, ((0, 4),))
    ln1_gain = jnp.clip(1.0 + 0.1 * jax.random.normal(splits[8], (D,), jnp.float32), 0.5, 1.5).astype(jnp.bfloat16)
    ln1_bias = normal_values(splits[9], (D,), 0.3, 1.5, ((0, 4),))
    ln2_gain = jnp.clip(1.0 + 0.1 * jax.random.normal(splits[10], (D,), jnp.float32), 0.5, 1.5).astype(jnp.bfloat16)
    ln2_bias = normal_values(splits[11], (D,), 0.3, 1.5, ((0, 4),))
    w_up = normal_values(splits[12], (D, FF), D ** -0.5, 0.21875, ((0, 4),))
    bias_up = normal_values(splits[13], (FF,), 0.3, 1.5, ((0, 4),))
    w_down = normal_values(splits[14], (FF, D), FF ** -0.5, 0.109375, ((0, 4),))
    bias_down = normal_values(splits[15], (D,), 0.3, 1.5, ((0, 4),))
    return {"tokens": tokens, "cotangent": cotangent, "segment": segment, "w_qkv": w_qkv, "bias_query": bias_query, "bias_value": bias_value, "w_out": w_out, "bias_out": bias_out, "ln1_gain": ln1_gain, "ln1_bias": ln1_bias, "ln2_gain": ln2_gain, "ln2_bias": ln2_bias, "w_up": w_up, "bias_up": bias_up, "w_down": w_down, "bias_down": bias_down}


@jax.custom_vjp
def low(v):
    return lax.optimization_barrier(v.astype(jnp.bfloat16)).astype(jnp.float32)

@jax.custom_vjp
def low_back(v):
    return v

def low_keep(v):
    return (low(v), None)

def low_pass(kept, grad):
    return (grad,)

def back_keep(v):
    return (v, None)

def back_low(kept, grad):
    return (low(grad),)
low.defvjp(low_keep, low_pass)
low_back.defvjp(back_keep, back_low)
highest = lax.Precision.HIGHEST
norm_eps = 1e-05
masked_value = -1e+30

def layer_norm(values, gain, offset):
    centre = lax.optimization_barrier(jnp.mean(values, axis=-1, keepdims=True))
    centred = values - centre
    variance = lax.optimization_barrier(jnp.mean(centred * centred, axis=-1, keepdims=True))
    return centred * lax.rsqrt(variance + norm_eps) * gain + offset

def product(left, right):
    return jnp.dot(left, right, precision=highest, preferred_element_type=jnp.float32)

def attention(queries, keys_values, segment):
    reach = LOOK * TOK_DEV
    window = (LOOK + 1) * TOK_DEV
    score_scale = HD ** (-0.5)
    padded = jnp.concatenate([jnp.zeros((reach, 2 * D), jnp.float32), keys_values], axis=0)
    padded_seg = jnp.concatenate([jnp.full((reach,), -1, jnp.int32), segment.astype(jnp.int32)])

    def one_block(start):
        start = start.astype(jnp.int32)
        block_q = lax.dynamic_slice_in_dim(queries, start, TOK_DEV, 0).reshape(TOK_DEV, H, HD)
        block_kv = lax.dynamic_slice_in_dim(padded, start, window, 0)
        block_k = block_kv[:, :D].reshape(window, H, HD)
        block_v = block_kv[:, D:].reshape(window, H, HD)
        query_seg = lax.dynamic_slice_in_dim(segment.astype(jnp.int32), start, TOK_DEV, 0)
        key_seg = lax.dynamic_slice_in_dim(padded_seg, start, window, 0)
        query_pos = start + jnp.arange(TOK_DEV, dtype=jnp.int32)
        key_pos = start - reach + jnp.arange(window, dtype=jnp.int32)
        allowed = (query_seg[:, None] == key_seg[None, :]) & (key_pos[None, :] <= query_pos[:, None]) & (key_pos[None, :] >= 0)
        raw = jnp.einsum('qhd,khd->hqk', block_q, block_k, precision=highest) * score_scale
        scores = low_back(raw)
        masked = jnp.where(allowed[None], scores, masked_value)
        totals = jax.nn.logsumexp(masked, axis=-1, keepdims=True)
        weights = jnp.where(allowed[None], jnp.exp(scores - totals), 0.0)
        mixed = jnp.einsum('hqk,khd->qhd', low(weights), block_v, precision=highest)
        return mixed.reshape(TOK_DEV, D)
    starts = jnp.arange(TOKENS // TOK_DEV, dtype=jnp.int32) * TOK_DEV
    return lax.map(jax.checkpoint(one_block), starts).reshape(TOKENS, D)

def reference(tokens, cotangent, segment, w_qkv, bias_query, bias_value, w_out, bias_out, ln1_gain, ln1_bias, ln2_gain, ln2_bias, w_up, bias_up, w_down, bias_down):

    def forward(inputs, qkv_weight, query_bias, value_bias, out_weight, out_bias, gain_one, offset_one, gain_two, offset_two, up_weight, up_bias, down_weight, down_bias):
        normed = low(layer_norm(inputs, gain_one, offset_one))
        joined_bias = jnp.concatenate([query_bias, jnp.zeros_like(query_bias), value_bias])
        projected = low(low_back(product(normed, qkv_weight) + joined_bias))
        mixed = low(low_back(attention(projected[:, :D], projected[:, D:], segment)))
        middle = inputs + low_back(product(mixed, out_weight) + out_bias)
        second = low(layer_norm(middle, gain_two, offset_two))
        hidden = low_back(product(second, up_weight) + up_bias)
        active = low(jax.nn.gelu(hidden, approximate=True))
        return middle + product(active, down_weight) + down_bias
    floats = [array.astype(jnp.float32) for array in (tokens, w_qkv, bias_query, bias_value, w_out, bias_out, ln1_gain, ln1_bias, ln2_gain, ln2_bias, w_up, bias_up, w_down, bias_down)]
    layer_out, pullback = jax.vjp(forward, *floats)
    grads = pullback(cotangent.astype(jnp.float32))
    return (layer_out, grads[0], grads[1], grads[2], grads[3], grads[4], grads[5], grads[6], grads[7], grads[8], grads[9], grads[10], grads[11], grads[12], grads[13])
```

```python
import functools

import jax
import jax.numpy as jnp
from jax import lax
from jax.experimental import pallas as pl
from jax.experimental.pallas import tpu as pltpu
from jax.sharding import PartitionSpec as P

H = 12
GROUP = 8
TILE = 256

norm_eps = 1e-05
masked_value = -1e30


def layer_norm(values, gain, offset):
    centre = jnp.mean(values, axis=-1, keepdims=True)
    centred = values - centre
    variance = jnp.mean(centred * centred, axis=-1, keepdims=True)
    return centred * lax.rsqrt(variance + norm_eps) * gain + offset


def gelu_tanh(values):
    return jax.nn.gelu(values, approximate=True)


def dot(left, right, left_dim, right_dim):
    return lax.dot_general(
        left, right, (((left_dim,), (right_dim,)), ((), ())), preferred_element_type=jnp.float32
    )


def exchange_kernel(source, target, send_sem, recv_sem, local_sem):
    rep = lax.axis_index("rep")
    shard = lax.axis_index("shard")
    across = GROUP // 4
    base = rep // across * across
    me = (rep - base) * 4 + shard

    def place(index):
        return (base + index // 4, lax.rem(index, 4))

    barrier = pltpu.get_barrier_semaphore()
    for step in range(1, GROUP):
        pl.semaphore_signal(
            barrier,
            inc=1,
            device_id=place(lax.rem(me + step, GROUP)),
            device_id_type=pl.DeviceIdType.MESH,
        )
    pl.semaphore_wait(barrier, GROUP - 1)
    own = pltpu.make_async_copy(source.at[me], target.at[me], local_sem)
    own.start()
    copies = []
    for step in range(1, GROUP):
        peer = lax.rem(me + step, GROUP)
        copy = pltpu.make_async_remote_copy(
            src_ref=source.at[peer],
            dst_ref=target.at[me],
            send_sem=send_sem.at[step],
            recv_sem=recv_sem.at[step],
            device_id=place(peer),
            device_id_type=pl.DeviceIdType.MESH,
        )
        copy.start()
        copies.append(copy)
    own.wait()
    for copy in copies:
        copy.wait()


def exchange(blocks, number):
    return pl.pallas_call(
        exchange_kernel,
        out_shape=jax.ShapeDtypeStruct(blocks.shape, blocks.dtype),
        in_specs=[pl.BlockSpec(memory_space=pl.ANY)],
        out_specs=pl.BlockSpec(memory_space=pl.ANY),
        scratch_shapes=[
            pltpu.SemaphoreType.DMA((GROUP,)),
            pltpu.SemaphoreType.DMA((GROUP,)),
            pltpu.SemaphoreType.DMA,
        ],
        compiler_params=pltpu.CompilerParams(collective_id=number, has_side_effects=True),
        name="exchange",
    )(blocks)


def tile_mask(chunk, first_row, last_row):
    key_pos = chunk * TILE + lax.broadcasted_iota(jnp.int32, (TILE, TILE), 0)
    return (key_pos >= first_row) & (key_pos <= last_row)


def chunk_lanes(chunk, offset):
    return pl.ds(pl.multiple_of(lax.rem(chunk, 2) * TILE + offset, TILE), TILE)


def attend_kernel(heads, size, low_ref, high_ref, first_ref, last_ref, pack_ref, out_ref, lse_ref):
    step = pl.program_id(0)
    rows = pack_ref.shape[2] - TILE
    half = rows // 2
    first_row, last_row = first_ref[0], last_ref[0]
    high = high_ref[step]
    queries = [
        pack_ref[step, h * size : (h + 1) * size, rows:] * (size**-0.5) for h in range(heads)
    ]

    def work(turn, carry):
        chunk = high - turn
        block = chunk // 2
        mask = tile_mask(chunk, first_row, last_row)
        result = []
        for h in range(heads):
            top, total, mixed = carry[h]
            here = slice(h * size, (h + 1) * size)
            keys = pack_ref[block, here, chunk_lanes(chunk, 0)]
            values = pack_ref[block, here, chunk_lanes(chunk, half)]
            scores = jnp.where(mask, dot(keys, queries[h], 0, 0), masked_value)
            new_top = jnp.maximum(top, jnp.max(scores, axis=0, keepdims=True))
            fresh = jnp.exp(scores - new_top)
            fade = jnp.exp(top - new_top)
            total = total * fade + jnp.sum(fresh, axis=0, keepdims=True)
            mixed = mixed * fade + dot(values, fresh.astype(jnp.bfloat16), 1, 0)
            result.append((new_top, total, mixed))
        return tuple(result)

    start = tuple(
        (
            jnp.full((1, TILE), masked_value, jnp.float32),
            jnp.zeros((1, TILE), jnp.float32),
            jnp.zeros((size, TILE), jnp.float32),
        )
        for _ in range(heads)
    )
    done = lax.fori_loop(0, high - low_ref[step] + 1, work, start)
    for h in range(heads):
        top, total, mixed = done[h]
        out_ref[0, h * size : (h + 1) * size, :] = mixed / total
        lse_ref[0, h : h + 1, :] = top + jnp.log(total)


def attend(low, high, first, last, pack, heads, size):
    blocks, rows, lanes = pack.shape
    row_spec = pl.BlockSpec((1, 1, TILE), lambda i, *_: (i, 0, 0))
    return pl.pallas_call(
        functools.partial(attend_kernel, heads, size),
        out_shape=(
            jax.ShapeDtypeStruct((blocks, rows, TILE), jnp.float32),
            jax.ShapeDtypeStruct((blocks, 8, TILE), jnp.float32),
        ),
        grid_spec=pltpu.PrefetchScalarGridSpec(
            num_scalar_prefetch=2,
            grid=(blocks,),
            in_specs=[
                row_spec,
                row_spec,
                pl.BlockSpec((blocks, rows, lanes), lambda i, *_: (0, 0, 0)),
            ],
            out_specs=(
                pl.BlockSpec((1, rows, TILE), lambda i, *_: (i, 0, 0)),
                pl.BlockSpec((1, 8, TILE), lambda i, *_: (i, 0, 0)),
            ),
        ),
        compiler_params=pltpu.CompilerParams(vmem_limit_bytes=40 * 1024 * 1024),
        cost_estimate=pl.CostEstimate(
            flops=4 * heads * size * TILE * TILE * 40,
            bytes_accessed=pack.size * 2,
            transcendentals=heads * TILE * TILE * 40,
        ),
        name="attend",
    )(low, high, first, last, pack)


def attend_back_kernel(
    heads, size, low_ref, high_ref, first_ref, last_ref, pack_ref, slope_ref, mixed_ref, lse_ref,
    out_ref, total_ref,
):
    step = pl.program_id(0)
    rows = pack_ref.shape[2] - TILE
    half = rows // 2
    scale = size**-0.5
    first_row, last_row = first_ref[0], last_ref[0]
    high = high_ref[step]

    @pl.when(step == 0)
    def _():
        total_ref[...] = jnp.zeros_like(total_ref)

    places = [slice(h * size, (h + 1) * size) for h in range(heads)]
    queries = [pack_ref[step, here, rows:] * scale for here in places]
    incoming = [slope_ref[0, here, :] for here in places]
    row_dots = [
        jnp.sum(
            slope_ref[0, here, :].astype(jnp.float32) * mixed_ref[0, here, :], axis=0, keepdims=True
        )
        for here in places
    ]
    totals = [lse_ref[0, h : h + 1, :] for h in range(heads)]

    def work(turn, carry):
        chunk = high - turn
        block = chunk // 2
        mask = tile_mask(chunk, first_row, last_row)
        key_lanes, value_lanes = chunk_lanes(chunk, 0), chunk_lanes(chunk, half)
        result = []
        for h in range(heads):
            here = places[h]
            keys = pack_ref[block, here, key_lanes]
            values = pack_ref[block, here, value_lanes]
            scores = dot(keys, queries[h], 0, 0)
            weights = jnp.exp(jnp.where(mask, scores - totals[h], masked_value))
            slopes = dot(values, incoming[h], 0, 0)
            grad_scores = (weights * (slopes - row_dots[h])).astype(jnp.bfloat16)
            total_ref[block, here, value_lanes] += dot(
                incoming[h], weights.astype(jnp.bfloat16), 1, 1
            )
            total_ref[block, here, key_lanes] += dot(queries[h], grad_scores, 1, 1)
            result.append(carry[h] + dot(keys, grad_scores, 1, 0))
        return tuple(result)

    start = tuple(jnp.zeros((size, TILE), jnp.float32) for _ in range(heads))
    done = lax.fori_loop(0, high - low_ref[step] + 1, work, start)
    for h in range(heads):
        out_ref[step, places[h], rows:] = (done[h] * scale).astype(out_ref.dtype)

    @pl.when(step == pl.num_programs(0) - 1)
    def _():
        for block in range(out_ref.shape[0]):
            out_ref[block, :, :rows] = total_ref[block].astype(out_ref.dtype)


def attend_back(low, high, first, last, pack, slope, mixed, lse, heads, size):
    blocks, rows, lanes = pack.shape
    row_spec = pl.BlockSpec((1, 1, TILE), lambda i, *_: (i, 0, 0))
    whole = pl.BlockSpec((blocks, rows, lanes), lambda i, *_: (0, 0, 0))
    tile_spec = pl.BlockSpec((1, rows, TILE), lambda i, *_: (i, 0, 0))
    return pl.pallas_call(
        functools.partial(attend_back_kernel, heads, size),
        out_shape=jax.ShapeDtypeStruct(pack.shape, jnp.bfloat16),
        grid_spec=pltpu.PrefetchScalarGridSpec(
            num_scalar_prefetch=2,
            grid=(blocks,),
            in_specs=[
                row_spec,
                row_spec,
                whole,
                tile_spec,
                tile_spec,
                pl.BlockSpec((1, 8, TILE), lambda i, *_: (i, 0, 0)),
            ],
            out_specs=whole,
            scratch_shapes=[pltpu.VMEM((blocks, rows, lanes - TILE), jnp.float32)],
        ),
        compiler_params=pltpu.CompilerParams(vmem_limit_bytes=40 * 1024 * 1024),
        cost_estimate=pl.CostEstimate(
            flops=10 * heads * size * TILE * TILE * 40,
            bytes_accessed=pack.size * 4,
            transcendentals=heads * TILE * TILE * 40,
        ),
        name="attend_back",
    )(low, high, first, last, pack, slope, mixed, lse)


def reduce_weight(grad):
    part = lax.psum_scatter(
        grad.astype(jnp.bfloat16), "shard", scatter_dimension=0, tiled=True
    )
    count = lax.axis_size("rep")
    rows, columns = part.shape
    part = lax.psum_scatter(
        part.reshape(count, rows * columns // count // 768, 768), "rep", scatter_dimension=0,
        tiled=False,
    )
    return lax.all_gather(part, "rep", axis=0, tiled=False).reshape(rows, columns)


def body(
    tokens,
    cotangent,
    segment,
    w_qkv,
    bias_query,
    bias_value,
    w_out,
    bias_out,
    ln1_gain,
    ln1_bias,
    ln2_gain,
    ln2_bias,
    w_up,
    bias_up,
    w_down,
    bias_down,
):
    f32, bf16 = jnp.float32, jnp.bfloat16
    small = (
        bias_query, bias_value, bias_out, ln1_gain, ln1_bias, ln2_gain, ln2_bias, bias_down, bias_up,
    )
    sizes = [value.shape[0] for value in small]
    joined = lax.all_gather(jnp.concatenate(small), "shard", axis=0, tiled=False)
    full_small = []
    at = 0
    for length in sizes:
        full_small.append(joined[:, at : at + length].reshape(-1).astype(f32))
        at += length
    (
        query_bias, value_bias, out_bias, gain_one, offset_one, gain_two, offset_two, down_bias, up_bias,
    ) = full_small
    full_qkv = lax.all_gather(w_qkv, "shard", axis=0, tiled=True)
    full_wout = lax.all_gather(w_out, "shard", axis=0, tiled=True)
    full_wup = lax.all_gather(w_up, "shard", axis=0, tiled=True)
    full_wdown = lax.all_gather(w_down, "shard", axis=0, tiled=True)

    tok_rows, width = tokens.shape
    size = width // H
    shards = lax.axis_size("shard")
    heads = H // shards
    part = heads * size
    rep, shard = lax.axis_index("rep"), lax.axis_index("shard")
    halves = GROUP // shards
    side = lax.rem(rep, halves)
    parity = lax.rem(shard, 2)

    span = GROUP * tok_rows
    group_seg = lax.dynamic_slice_in_dim(segment, rep // halves * span, span, 0)
    one = jnp.sum((group_seg == group_seg[0]).astype(jnp.int32))
    two = span - jnp.sum((group_seg == group_seg[span - 1]).astype(jnp.int32))
    blocks = jnp.arange(GROUP, dtype=jnp.int32)
    high = 2 * blocks + jnp.where(blocks % 2 == 0, side, 1 - side)
    last = high[:, None] * TILE + jnp.arange(TILE, dtype=jnp.int32)[None, :]
    first = jnp.where(last >= two, two, jnp.where(last >= one, one, 0))
    low = first[:, 0] // TILE
    first, last = first[:, None, :], last[:, None, :]

    inputs = tokens.astype(f32)
    normed, norm_one_back = jax.vjp(layer_norm, inputs, gain_one, offset_one)
    normed_low = normed.astype(bf16)
    joined_bias = jnp.concatenate([query_bias, jnp.zeros_like(query_bias), value_bias])
    projected = (dot(full_qkv, normed_low, 0, 1) + joined_bias[:, None]).astype(bf16)
    parts = projected.reshape(3, shards, part, tok_rows)

    def by_side(value):
        near, far = value[..., :TILE], value[..., TILE:]
        swap = parity == 1
        return jnp.stack([jnp.where(swap, far, near), jnp.where(swap, near, far)], axis=0)

    def by_token(value):
        swap = parity == 1
        return jnp.concatenate(
            [jnp.where(swap, value[1], value[0]), jnp.where(swap, value[0], value[1])], axis=-1
        )

    pairs = jnp.concatenate([parts[1], parts[2]], axis=-1)
    message = jnp.concatenate(
        [jnp.broadcast_to(pairs[None], (halves,) + pairs.shape), by_side(parts[0])], axis=-1
    ).reshape(GROUP, part, 2 * tok_rows + TILE)
    pack = exchange(message, 1)
    mixed_tiles, lse = attend(low, high, first, last, pack, heads, size)
    back = exchange(mixed_tiles.astype(bf16), 2)
    mixed_low = by_token(back.reshape(halves, shards, part, TILE)).reshape(width, tok_rows)

    middle = inputs + dot(mixed_low, full_wout, 0, 0) + out_bias
    second, norm_two_back = jax.vjp(layer_norm, middle, gain_two, offset_two)
    second_low = second.astype(bf16)
    hidden = dot(second_low, full_wup, 1, 0) + up_bias
    active, gelu_back = jax.vjp(gelu_tanh, hidden)
    active_low = active.astype(bf16)
    layer_out = middle + dot(active_low, full_wdown, 1, 0) + down_bias
    grad_out = cotangent.astype(f32)
    grad_wdown = reduce_weight(dot(active_low, cotangent, 0, 0))
    grad_down_bias = jnp.sum(grad_out, axis=0)
    (grad_hidden,) = gelu_back(dot(cotangent, full_wdown, 1, 1))
    hidden_low = grad_hidden.astype(bf16)
    grad_wup = reduce_weight(dot(second_low, hidden_low, 0, 0))
    grad_up_bias = jnp.sum(hidden_low.astype(f32), axis=0)
    grad_second = dot(hidden_low, full_wup, 1, 1)
    grad_middle_norm, grad_gain_two, grad_offset_two = norm_two_back(grad_second)
    grad_middle = grad_out + grad_middle_norm
    middle_low = grad_middle.astype(bf16)
    grad_wout = reduce_weight(dot(mixed_low, middle_low, 1, 0))
    grad_out_bias = jnp.sum(middle_low.astype(f32), axis=0)
    grad_mixed = dot(full_wout, middle_low, 1, 1).astype(bf16)

    slope = exchange(
        by_side(grad_mixed.reshape(shards, part, tok_rows)).reshape(GROUP, part, TILE), 3
    )
    grad_pack = attend_back(low, high, first, last, pack, slope, mixed_tiles, lse, heads, size)
    returned = exchange(grad_pack, 4).reshape(halves, shards, part, 2 * tok_rows + TILE)
    grad_pairs = jnp.sum(returned[..., : 2 * tok_rows].astype(f32), axis=0).astype(bf16)
    grad_projected = jnp.stack(
        [
            by_token(returned[..., 2 * tok_rows :]),
            grad_pairs[..., :tok_rows],
            grad_pairs[..., tok_rows:],
        ],
        axis=0,
    ).reshape(3 * width, tok_rows)
    grad_wqkv = reduce_weight(dot(normed_low, grad_projected, 0, 1))
    bias_grads = jnp.sum(grad_projected.astype(f32), axis=1)
    grad_query_bias = bias_grads[:width]
    grad_value_bias = bias_grads[2 * width :]
    grad_normed = dot(grad_projected, full_qkv, 0, 1)
    grad_input_norm, grad_gain_one, grad_offset_one = norm_one_back(grad_normed)
    grad_input = grad_middle + grad_input_norm

    small_grads = (
        grad_query_bias, grad_value_bias, grad_out_bias, grad_gain_one, grad_offset_one,
        grad_gain_two, grad_offset_two, grad_down_bias, grad_up_bias,
    )
    laid = jnp.concatenate([value.reshape(shards, -1) for value in small_grads], axis=1)
    summed = lax.dynamic_index_in_dim(
        lax.psum(laid, ("rep", "shard")), shard, 0, keepdims=False
    )
    pieces = []
    at = 0
    for length in sizes:
        pieces.append(summed[at : at + length])
        at += length
    (
        sum_query_bias, sum_value_bias, sum_out_bias, sum_gain_one, sum_offset_one, sum_gain_two,
        sum_offset_two, sum_down_bias, sum_up_bias,
    ) = pieces
    return (
        layer_out,
        grad_input,
        grad_wqkv.astype(f32),
        sum_query_bias,
        sum_value_bias,
        grad_wout.astype(f32),
        sum_out_bias,
        sum_gain_one,
        sum_offset_one,
        sum_gain_two,
        sum_offset_two,
        grad_wup.astype(f32),
        sum_up_bias,
        grad_wdown.astype(f32),
        sum_down_bias,
    )


def solution(mesh):
    tokens_at, rows_at, vector_at = P(("rep", "shard"), None), P("shard", None), P("shard")
    return jax.shard_map(
        body,
        mesh=mesh,
        in_specs=(
            tokens_at, tokens_at, P(), rows_at, vector_at, vector_at, rows_at, vector_at, vector_at,
            vector_at, vector_at, vector_at, rows_at, vector_at, rows_at, vector_at,
        ),
        out_specs=(
            tokens_at, tokens_at, rows_at, vector_at, vector_at, rows_at, vector_at, vector_at,
            vector_at, vector_at, vector_at, rows_at, vector_at, rows_at, vector_at,
        ),
        check_vma=False,
    )
```

```python
import functools

import jax
import jax.numpy as jnp
from jax import lax
from jax.experimental import pallas as pl
from jax.experimental.pallas import tpu as pltpu
from jax.sharding import PartitionSpec as P

H = 12
GROUP = 8
TILE = 256

norm_eps = 1e-05
masked_value = -1e30


def layer_norm(values, gain, offset):
    centre = jnp.mean(values, axis=-1, keepdims=True)
    centred = values - centre
    variance = jnp.mean(centred * centred, axis=-1, keepdims=True)
    return centred * lax.rsqrt(variance + norm_eps) * gain + offset


def gelu_tanh(values):
    return jax.nn.gelu(values, approximate=True)


def dot(left, right, left_dim, right_dim):
    return lax.dot_general(
        left, right, (((left_dim,), (right_dim,)), ((), ())), preferred_element_type=jnp.float32
    )


def exchange_kernel(source, target, send_sem, recv_sem, local_sem):
    rep = lax.axis_index("rep")
    shard = lax.axis_index("shard")
    across = GROUP // 4
    base = rep // across * across
    me = (rep - base) * 4 + shard

    def place(index):
        return (base + index // 4, lax.rem(index, 4))

    barrier = pltpu.get_barrier_semaphore()
    for step in range(1, GROUP):
        pl.semaphore_signal(
            barrier,
            inc=1,
            device_id=place(lax.rem(me + step, GROUP)),
            device_id_type=pl.DeviceIdType.MESH,
        )
    pl.semaphore_wait(barrier, GROUP - 1)
    own = pltpu.make_async_copy(source.at[me], target.at[me], local_sem)
    own.start()
    copies = []
    for step in range(1, GROUP):
        peer = lax.rem(me + step, GROUP)
        copy = pltpu.make_async_remote_copy(
            src_ref=source.at[peer],
            dst_ref=target.at[me],
            send_sem=send_sem.at[step],
            recv_sem=recv_sem.at[step],
            device_id=place(peer),
            device_id_type=pl.DeviceIdType.MESH,
        )
        copy.start()
        copies.append(copy)
    own.wait()
    for copy in copies:
        copy.wait()


def exchange(blocks, number):
    return pl.pallas_call(
        exchange_kernel,
        out_shape=jax.ShapeDtypeStruct(blocks.shape, blocks.dtype),
        in_specs=[pl.BlockSpec(memory_space=pl.ANY)],
        out_specs=pl.BlockSpec(memory_space=pl.ANY),
        scratch_shapes=[
            pltpu.SemaphoreType.DMA((GROUP,)),
            pltpu.SemaphoreType.DMA((GROUP,)),
            pltpu.SemaphoreType.DMA,
        ],
        compiler_params=pltpu.CompilerParams(collective_id=number, has_side_effects=True),
        name="exchange",
    )(blocks)


def tile_mask(chunk, first_row, last_row):
    key_pos = chunk * TILE + lax.broadcasted_iota(jnp.int32, (TILE, TILE), 0)
    return (key_pos >= first_row) & (key_pos <= last_row)


def chunk_lanes(chunk, offset):
    return pl.ds(pl.multiple_of(lax.rem(chunk, 2) * TILE + offset, TILE), TILE)


def attend_kernel(heads, size, low_ref, high_ref, first_ref, last_ref, pack_ref, out_ref, lse_ref):
    step = pl.program_id(0)
    rows = pack_ref.shape[2] - TILE
    half = rows // 2
    first_row, last_row = first_ref[0], last_ref[0]
    high = high_ref[step]
    queries = [
        pack_ref[step, h * size : (h + 1) * size, rows:] * (size**-0.5) for h in range(heads)
    ]

    def work(turn, carry):
        chunk = high - turn
        block = chunk // 2
        mask = tile_mask(chunk, first_row, last_row)
        result = []
        for h in range(heads):
            top, total, mixed = carry[h]
            here = slice(h * size, (h + 1) * size)
            keys = pack_ref[block, here, chunk_lanes(chunk, 0)]
            values = pack_ref[block, here, chunk_lanes(chunk, half)]
            scores = jnp.where(mask, dot(keys, queries[h], 0, 0), masked_value)
            new_top = jnp.maximum(top, jnp.max(scores, axis=0, keepdims=True))
            fresh = jnp.exp(scores - new_top)
            fade = jnp.exp(top - new_top)
            total = total * fade + jnp.sum(fresh, axis=0, keepdims=True)
            mixed = mixed * fade + dot(values, fresh.astype(jnp.bfloat16), 1, 0)
            result.append((new_top, total, mixed))
        return tuple(result)

    start = tuple(
        (
            jnp.full((1, TILE), masked_value, jnp.float32),
            jnp.zeros((1, TILE), jnp.float32),
            jnp.zeros((size, TILE), jnp.float32),
        )
        for _ in range(heads)
    )
    done = lax.fori_loop(0, high - low_ref[step] + 1, work, start)
    for h in range(heads):
        top, total, mixed = done[h]
        out_ref[0, h * size : (h + 1) * size, :] = mixed / total
        lse_ref[0, h : h + 1, :] = top + jnp.log(total)


def attend(low, high, first, last, pack, heads, size):
    blocks, rows, lanes = pack.shape
    row_spec = pl.BlockSpec((1, 1, TILE), lambda i, *_: (i, 0, 0))
    return pl.pallas_call(
        functools.partial(attend_kernel, heads, size),
        out_shape=(
            jax.ShapeDtypeStruct((blocks, rows, TILE), jnp.float32),
            jax.ShapeDtypeStruct((blocks, 8, TILE), jnp.float32),
        ),
        grid_spec=pltpu.PrefetchScalarGridSpec(
            num_scalar_prefetch=2,
            grid=(blocks,),
            in_specs=[
                row_spec,
                row_spec,
                pl.BlockSpec((blocks, rows, lanes), lambda i, *_: (0, 0, 0)),
            ],
            out_specs=(
                pl.BlockSpec((1, rows, TILE), lambda i, *_: (i, 0, 0)),
                pl.BlockSpec((1, 8, TILE), lambda i, *_: (i, 0, 0)),
            ),
        ),
        compiler_params=pltpu.CompilerParams(vmem_limit_bytes=40 * 1024 * 1024),
        cost_estimate=pl.CostEstimate(
            flops=4 * heads * size * TILE * TILE * 40,
            bytes_accessed=pack.size * 2,
            transcendentals=heads * TILE * TILE * 40,
        ),
        name="attend",
    )(low, high, first, last, pack)


def attend_back_kernel(
    heads, size, low_ref, high_ref, first_ref, last_ref, pack_ref, slope_ref, mixed_ref, lse_ref,
    out_ref, total_ref,
):
    step = pl.program_id(0)
    rows = pack_ref.shape[2] - TILE
    half = rows // 2
    scale = size**-0.5
    first_row, last_row = first_ref[0], last_ref[0]
    high = high_ref[step]

    @pl.when(step == 0)
    def _():
        total_ref[...] = jnp.zeros_like(total_ref)

    places = [slice(h * size, (h + 1) * size) for h in range(heads)]
    queries = [pack_ref[step, here, rows:] * scale for here in places]
    incoming = [slope_ref[0, here, :] for here in places]
    row_dots = [
        jnp.sum(
            slope_ref[0, here, :].astype(jnp.float32) * mixed_ref[0, here, :], axis=0, keepdims=True
        )
        for here in places
    ]
    totals = [lse_ref[0, h : h + 1, :] for h in range(heads)]

    def work(turn, carry):
        chunk = high - turn
        block = chunk // 2
        mask = tile_mask(chunk, first_row, last_row)
        key_lanes, value_lanes = chunk_lanes(chunk, 0), chunk_lanes(chunk, half)
        result = []
        for h in range(heads):
            here = places[h]
            keys = pack_ref[block, here, key_lanes]
            values = pack_ref[block, here, value_lanes]
            scores = dot(keys, queries[h], 0, 0)
            weights = jnp.exp(jnp.where(mask, scores - totals[h], masked_value))
            slopes = dot(values, incoming[h], 0, 0)
            grad_scores = (weights * (slopes - row_dots[h])).astype(jnp.bfloat16)
            total_ref[block, here, value_lanes] += dot(
                incoming[h], weights.astype(jnp.bfloat16), 1, 1
            )
            total_ref[block, here, key_lanes] += dot(queries[h], grad_scores, 1, 1)
            result.append(carry[h] + dot(keys, grad_scores, 1, 0))
        return tuple(result)

    start = tuple(jnp.zeros((size, TILE), jnp.float32) for _ in range(heads))
    done = lax.fori_loop(0, high - low_ref[step] + 1, work, start)
    for h in range(heads):
        out_ref[step, places[h], rows:] = (done[h] * scale).astype(out_ref.dtype)

    @pl.when(step == pl.num_programs(0) - 1)
    def _():
        for block in range(out_ref.shape[0]):
            out_ref[block, :, :rows] = total_ref[block].astype(out_ref.dtype)


def attend_back(low, high, first, last, pack, slope, mixed, lse, heads, size):
    blocks, rows, lanes = pack.shape
    row_spec = pl.BlockSpec((1, 1, TILE), lambda i, *_: (i, 0, 0))
    whole = pl.BlockSpec((blocks, rows, lanes), lambda i, *_: (0, 0, 0))
    tile_spec = pl.BlockSpec((1, rows, TILE), lambda i, *_: (i, 0, 0))
    return pl.pallas_call(
        functools.partial(attend_back_kernel, heads, size),
        out_shape=jax.ShapeDtypeStruct(pack.shape, jnp.bfloat16),
        grid_spec=pltpu.PrefetchScalarGridSpec(
            num_scalar_prefetch=2,
            grid=(blocks,),
            in_specs=[
                row_spec,
                row_spec,
                whole,
                tile_spec,
                tile_spec,
                pl.BlockSpec((1, 8, TILE), lambda i, *_: (i, 0, 0)),
            ],
            out_specs=whole,
            scratch_shapes=[pltpu.VMEM((blocks, rows, lanes - TILE), jnp.float32)],
        ),
        compiler_params=pltpu.CompilerParams(vmem_limit_bytes=40 * 1024 * 1024),
        cost_estimate=pl.CostEstimate(
            flops=10 * heads * size * TILE * TILE * 40,
            bytes_accessed=pack.size * 4,
            transcendentals=heads * TILE * TILE * 40,
        ),
        name="attend_back",
    )(low, high, first, last, pack, slope, mixed, lse)


def swap_with(value, bit):
    count = lax.axis_size(("rep", "shard"))
    return lax.ppermute(
        value, ("rep", "shard"), [(index, index ^ (1 << bit)) for index in range(count)]
    )


def bit_of(index, bit):
    return lax.rem(index // (1 << bit), 2)


def reduce_weight(grad, pieces=1, turned=False):
    count = lax.axis_size(("rep", "shard"))
    bits = count.bit_length() - 1
    shards = lax.axis_size("shard")
    shard_bits = shards.bit_length() - 1
    index = lax.axis_index("rep") * shards + lax.axis_index("shard")
    rows, columns = grad.shape
    lanes = 768 // pieces
    names = list(range(shard_bits - 1, -1, -1)) + list(range(bits - 1, shard_bits - 1, -1))
    parts = grad.astype(jnp.bfloat16).reshape(
        (2,) * bits + (rows * columns // count // 768, pieces, lanes)
    )
    done = []
    for piece in range(pieces):
        part = parts[..., piece, :]
        left = list(names)
        order = list(range(bits))
        if (piece % 2 == 1) != turned:
            order[1:3] = order[2:0:-1]
        for bit in order:
            axis = left.index(bit)
            mine = bit_of(index, bit)
            keep = lax.dynamic_index_in_dim(part, mine, axis, keepdims=False)
            give = lax.dynamic_index_in_dim(part, 1 - mine, axis, keepdims=False)
            came = swap_with(give, bit)
            part = (keep.astype(jnp.float32) + came.astype(jnp.float32)).astype(jnp.bfloat16)
            left.remove(bit)
        for bit in range(bits - 1, shard_bits - 1, -1):
            came = swap_with(part, bit)
            mine = bit_of(index, bit)
            axis = bits - 1 - bit
            low = jnp.where(mine == 0, part, came)
            high = jnp.where(mine == 0, came, part)
            part = jnp.stack([low, high], axis=axis)
        done.append(part)
    whole = jnp.stack(done, axis=-2) if pieces > 1 else done[0]
    return whole.reshape(rows // shards, columns)


def reduce_small(value):
    for bit in range(lax.axis_size(("rep", "shard")).bit_length() - 1):
        value = value + swap_with(value, bit)
    return value


def body(
    tokens,
    cotangent,
    segment,
    w_qkv,
    bias_query,
    bias_value,
    w_out,
    bias_out,
    ln1_gain,
    ln1_bias,
    ln2_gain,
    ln2_bias,
    w_up,
    bias_up,
    w_down,
    bias_down,
):
    f32, bf16 = jnp.float32, jnp.bfloat16
    small = (
        bias_query, bias_value, bias_out, ln1_gain, ln1_bias, ln2_gain, ln2_bias, bias_down, bias_up,
    )
    sizes = [value.shape[0] for value in small]
    joined = lax.all_gather(jnp.concatenate(small), "shard", axis=0, tiled=False)
    full_small = []
    at = 0
    for length in sizes:
        full_small.append(joined[:, at : at + length].reshape(-1).astype(f32))
        at += length
    (
        query_bias, value_bias, out_bias, gain_one, offset_one, gain_two, offset_two, down_bias, up_bias,
    ) = full_small
    full_qkv = lax.all_gather(w_qkv, "shard", axis=0, tiled=True)
    full_wout = lax.all_gather(w_out, "shard", axis=0, tiled=True)
    full_wup = lax.all_gather(w_up, "shard", axis=0, tiled=True)
    full_wdown = lax.all_gather(w_down, "shard", axis=0, tiled=True)

    tok_rows, width = tokens.shape
    size = width // H
    shards = lax.axis_size("shard")
    heads = H // shards
    part = heads * size
    rep, shard = lax.axis_index("rep"), lax.axis_index("shard")
    halves = GROUP // shards
    side = lax.rem(rep, halves)
    parity = lax.rem(shard, 2)

    span = GROUP * tok_rows
    group_seg = lax.dynamic_slice_in_dim(segment, rep // halves * span, span, 0)
    one = jnp.sum((group_seg == group_seg[0]).astype(jnp.int32))
    two = span - jnp.sum((group_seg == group_seg[span - 1]).astype(jnp.int32))
    blocks = jnp.arange(GROUP, dtype=jnp.int32)
    high = 2 * blocks + jnp.where(blocks % 2 == 0, side, 1 - side)
    last = high[:, None] * TILE + jnp.arange(TILE, dtype=jnp.int32)[None, :]
    first = jnp.where(last >= two, two, jnp.where(last >= one, one, 0))
    low = first[:, 0] // TILE
    first, last = first[:, None, :], last[:, None, :]

    inputs = tokens.astype(f32)
    normed, norm_one_back = jax.vjp(layer_norm, inputs, gain_one, offset_one)
    normed_low = normed.astype(bf16)
    joined_bias = jnp.concatenate([query_bias, jnp.zeros_like(query_bias), value_bias])
    projected = (dot(full_qkv, normed_low, 0, 1) + joined_bias[:, None]).astype(bf16)
    parts = projected.reshape(3, shards, part, tok_rows)

    def by_side(value):
        near, far = value[..., :TILE], value[..., TILE:]
        swap = parity == 1
        return jnp.stack([jnp.where(swap, far, near), jnp.where(swap, near, far)], axis=0)

    def by_token(value):
        swap = parity == 1
        return jnp.concatenate(
            [jnp.where(swap, value[1], value[0]), jnp.where(swap, value[0], value[1])], axis=-1
        )

    pairs = jnp.concatenate([parts[1], parts[2]], axis=-1)
    message = jnp.concatenate(
        [jnp.broadcast_to(pairs[None], (halves,) + pairs.shape), by_side(parts[0])], axis=-1
    ).reshape(GROUP, part, 2 * tok_rows + TILE)
    pack = exchange(message, 1)
    mixed_tiles, lse = attend(low, high, first, last, pack, heads, size)
    back = exchange(mixed_tiles.astype(bf16), 2)
    mixed_low = by_token(back.reshape(halves, shards, part, TILE)).reshape(width, tok_rows)

    middle = inputs + dot(mixed_low, full_wout, 0, 0) + out_bias
    second, norm_two_back = jax.vjp(layer_norm, middle, gain_two, offset_two)
    second_low = second.astype(bf16)
    hidden = dot(second_low, full_wup, 1, 0) + up_bias
    active, gelu_back = jax.vjp(gelu_tanh, hidden)
    active_low = active.astype(bf16)
    layer_out = middle + dot(active_low, full_wdown, 1, 0) + down_bias
    grad_out = cotangent.astype(f32)
    grad_wdown = reduce_weight(dot(active_low, cotangent, 0, 0))
    grad_down_bias = jnp.sum(grad_out, axis=0)
    (grad_hidden,) = gelu_back(dot(cotangent, full_wdown, 1, 1))
    hidden_low = grad_hidden.astype(bf16)
    grad_wup = reduce_weight(dot(second_low, hidden_low, 0, 0), 1, True)
    grad_up_bias = jnp.sum(hidden_low.astype(f32), axis=0)
    grad_second = dot(hidden_low, full_wup, 1, 1)
    grad_middle_norm, grad_gain_two, grad_offset_two = norm_two_back(grad_second)
    grad_middle = grad_out + grad_middle_norm
    middle_low = grad_middle.astype(bf16)
    grad_wout = reduce_weight(dot(mixed_low, middle_low, 1, 0))
    grad_out_bias = jnp.sum(middle_low.astype(f32), axis=0)
    grad_mixed = dot(full_wout, middle_low, 1, 1).astype(bf16)

    slope = exchange(
        by_side(grad_mixed.reshape(shards, part, tok_rows)).reshape(GROUP, part, TILE), 3
    )
    grad_pack = attend_back(low, high, first, last, pack, slope, mixed_tiles, lse, heads, size)
    returned = exchange(grad_pack, 4).reshape(halves, shards, part, 2 * tok_rows + TILE)
    grad_pairs = jnp.sum(returned[..., : 2 * tok_rows].astype(f32), axis=0).astype(bf16)
    grad_projected = jnp.stack(
        [
            by_token(returned[..., 2 * tok_rows :]),
            grad_pairs[..., :tok_rows],
            grad_pairs[..., tok_rows:],
        ],
        axis=0,
    ).reshape(3 * width, tok_rows)
    grad_wqkv = reduce_weight(dot(normed_low, grad_projected, 0, 1), 2)
    bias_grads = jnp.sum(grad_projected.astype(f32), axis=1)
    grad_query_bias = bias_grads[:width]
    grad_value_bias = bias_grads[2 * width :]
    grad_normed = dot(grad_projected, full_qkv, 0, 1)
    grad_input_norm, grad_gain_one, grad_offset_one = norm_one_back(grad_normed)
    grad_input = grad_middle + grad_input_norm

    small_grads = (
        grad_query_bias, grad_value_bias, grad_out_bias, grad_gain_one, grad_offset_one,
        grad_gain_two, grad_offset_two, grad_down_bias, grad_up_bias,
    )
    laid = jnp.concatenate([value.reshape(shards, -1) for value in small_grads], axis=1)
    summed = lax.dynamic_index_in_dim(
        reduce_small(laid), shard, 0, keepdims=False
    )
    pieces = []
    at = 0
    for length in sizes:
        pieces.append(summed[at : at + length])
        at += length
    (
        sum_query_bias, sum_value_bias, sum_out_bias, sum_gain_one, sum_offset_one, sum_gain_two,
        sum_offset_two, sum_down_bias, sum_up_bias,
    ) = pieces
    return (
        layer_out,
        grad_input,
        grad_wqkv.astype(f32),
        sum_query_bias,
        sum_value_bias,
        grad_wout.astype(f32),
        sum_out_bias,
        sum_gain_one,
        sum_offset_one,
        sum_gain_two,
        sum_offset_two,
        grad_wup.astype(f32),
        sum_up_bias,
        grad_wdown.astype(f32),
        sum_down_bias,
    )


def solution(mesh):
    tokens_at, rows_at, vector_at = P(("rep", "shard"), None), P("shard", None), P("shard")
    return jax.shard_map(
        body,
        mesh=mesh,
        in_specs=(
            tokens_at, tokens_at, P(), rows_at, vector_at, vector_at, rows_at, vector_at, vector_at,
            vector_at, vector_at, vector_at, rows_at, vector_at, rows_at, vector_at,
        ),
        out_specs=(
            tokens_at, tokens_at, rows_at, vector_at, vector_at, rows_at, vector_at, vector_at,
            vector_at, vector_at, vector_at, rows_at, vector_at, rows_at, vector_at,
        ),
        check_vma=False,
    )
```

```python
import functools

import jax
import jax.numpy as jnp
from jax import lax
from jax.experimental import pallas as pl
from jax.experimental.pallas import tpu as pltpu
from jax.sharding import PartitionSpec as P

H = 12
GROUP = 8
TILE = 256

norm_eps = 1e-05
masked_value = -1e30


def layer_norm(values, gain, offset):
    centre = jnp.mean(values, axis=-1, keepdims=True)
    centred = values - centre
    variance = jnp.mean(centred * centred, axis=-1, keepdims=True)
    return centred * lax.rsqrt(variance + norm_eps) * gain + offset


def gelu_tanh(values):
    return jax.nn.gelu(values, approximate=True)


def dot(left, right, left_dim, right_dim):
    return lax.dot_general(
        left, right, (((left_dim,), (right_dim,)), ((), ())), preferred_element_type=jnp.float32
    )


def exchange_kernel(source, *refs):
    target, send_sem, recv_sem, local_sem = refs[-4:]
    rep = lax.axis_index("rep")
    shard = lax.axis_index("shard")
    across = GROUP // 4
    base = rep // across * across
    me = (rep - base) * 4 + shard

    def place(index):
        return (base + index // 4, lax.rem(index, 4))

    barrier = pltpu.get_barrier_semaphore()
    for step in range(1, GROUP):
        pl.semaphore_signal(
            barrier,
            inc=1,
            device_id=place(lax.rem(me + step, GROUP)),
            device_id_type=pl.DeviceIdType.MESH,
        )
    pl.semaphore_wait(barrier, GROUP - 1)
    own = pltpu.make_async_copy(source.at[me], target.at[me], local_sem)
    own.start()
    copies = []
    for step in range(1, GROUP):
        peer = lax.rem(me + step, GROUP)
        copy = pltpu.make_async_remote_copy(
            src_ref=source.at[peer],
            dst_ref=target.at[me],
            send_sem=send_sem.at[step],
            recv_sem=recv_sem.at[step],
            device_id=place(peer),
            device_id_type=pl.DeviceIdType.MESH,
        )
        copy.start()
        copies.append(copy)
    own.wait()
    for copy in copies:
        copy.wait()


def exchange(blocks, number, *behind):
    return pl.pallas_call(
        exchange_kernel,
        out_shape=jax.ShapeDtypeStruct(blocks.shape, blocks.dtype),
        in_specs=[pl.BlockSpec(memory_space=pl.ANY)] * (1 + len(behind)),
        out_specs=pl.BlockSpec(memory_space=pl.ANY),
        scratch_shapes=[
            pltpu.SemaphoreType.DMA((GROUP,)),
            pltpu.SemaphoreType.DMA((GROUP,)),
            pltpu.SemaphoreType.DMA,
        ],
        compiler_params=pltpu.CompilerParams(collective_id=number, has_side_effects=True),
        name="exchange",
    )(blocks, *behind)


def tile_mask(chunk, first_row, last_row):
    key_pos = chunk * TILE + lax.broadcasted_iota(jnp.int32, (TILE, TILE), 0)
    return (key_pos >= first_row) & (key_pos <= last_row)


def chunk_lanes(chunk, offset):
    return pl.ds(pl.multiple_of(lax.rem(chunk, 2) * TILE + offset, TILE), TILE)


def attend_kernel(heads, size, low_ref, high_ref, first_ref, last_ref, pack_ref, out_ref, lse_ref):
    step = pl.program_id(0)
    rows = pack_ref.shape[2] - TILE
    half = rows // 2
    first_row, last_row = first_ref[0], last_ref[0]
    high = high_ref[step]
    queries = [
        pack_ref[step, h * size : (h + 1) * size, rows:] * (size**-0.5) for h in range(heads)
    ]

    def work(turn, carry):
        chunk = high - turn
        block = chunk // 2
        mask = tile_mask(chunk, first_row, last_row)
        result = []
        for h in range(heads):
            top, total, mixed = carry[h]
            here = slice(h * size, (h + 1) * size)
            keys = pack_ref[block, here, chunk_lanes(chunk, 0)]
            values = pack_ref[block, here, chunk_lanes(chunk, half)]
            scores = jnp.where(mask, dot(keys, queries[h], 0, 0), masked_value)
            new_top = jnp.maximum(top, jnp.max(scores, axis=0, keepdims=True))
            fresh = jnp.exp(scores - new_top)
            fade = jnp.exp(top - new_top)
            total = total * fade + jnp.sum(fresh, axis=0, keepdims=True)
            mixed = mixed * fade + dot(values, fresh.astype(jnp.bfloat16), 1, 0)
            result.append((new_top, total, mixed))
        return tuple(result)

    start = tuple(
        (
            jnp.full((1, TILE), masked_value, jnp.float32),
            jnp.zeros((1, TILE), jnp.float32),
            jnp.zeros((size, TILE), jnp.float32),
        )
        for _ in range(heads)
    )
    done = lax.fori_loop(0, high - low_ref[step] + 1, work, start)
    for h in range(heads):
        top, total, mixed = done[h]
        out_ref[0, h * size : (h + 1) * size, :] = mixed / total
        lse_ref[0, h : h + 1, :] = top + jnp.log(total)


def attend(low, high, first, last, pack, heads, size):
    blocks, rows, lanes = pack.shape
    row_spec = pl.BlockSpec((1, 1, TILE), lambda i, *_: (i, 0, 0))
    return pl.pallas_call(
        functools.partial(attend_kernel, heads, size),
        out_shape=(
            jax.ShapeDtypeStruct((blocks, rows, TILE), jnp.float32),
            jax.ShapeDtypeStruct((blocks, 8, TILE), jnp.float32),
        ),
        grid_spec=pltpu.PrefetchScalarGridSpec(
            num_scalar_prefetch=2,
            grid=(blocks,),
            in_specs=[
                row_spec,
                row_spec,
                pl.BlockSpec((blocks, rows, lanes), lambda i, *_: (0, 0, 0)),
            ],
            out_specs=(
                pl.BlockSpec((1, rows, TILE), lambda i, *_: (i, 0, 0)),
                pl.BlockSpec((1, 8, TILE), lambda i, *_: (i, 0, 0)),
            ),
        ),
        compiler_params=pltpu.CompilerParams(vmem_limit_bytes=40 * 1024 * 1024),
        cost_estimate=pl.CostEstimate(
            flops=4 * heads * size * TILE * TILE * 40,
            bytes_accessed=pack.size * 2,
            transcendentals=heads * TILE * TILE * 40,
        ),
        name="attend",
    )(low, high, first, last, pack)


def attend_back_kernel(
    heads, size, low_ref, high_ref, first_ref, last_ref, pack_ref, slope_ref, mixed_ref, lse_ref,
    *refs,
):
    out_ref, total_ref = refs[-2:]
    step = pl.program_id(0)
    rows = pack_ref.shape[2] - TILE
    half = rows // 2
    scale = size**-0.5
    first_row, last_row = first_ref[0], last_ref[0]
    high = high_ref[step]

    @pl.when(step == 0)
    def _():
        total_ref[...] = jnp.zeros_like(total_ref)

    places = [slice(h * size, (h + 1) * size) for h in range(heads)]
    queries = [pack_ref[step, here, rows:] * scale for here in places]
    incoming = [slope_ref[0, here, :] for here in places]
    row_dots = [
        jnp.sum(
            slope_ref[0, here, :].astype(jnp.float32) * mixed_ref[0, here, :], axis=0, keepdims=True
        )
        for here in places
    ]
    totals = [lse_ref[0, h : h + 1, :] for h in range(heads)]

    def work(turn, carry):
        chunk = high - turn
        block = chunk // 2
        mask = tile_mask(chunk, first_row, last_row)
        key_lanes, value_lanes = chunk_lanes(chunk, 0), chunk_lanes(chunk, half)
        result = []
        for h in range(heads):
            here = places[h]
            keys = pack_ref[block, here, key_lanes]
            values = pack_ref[block, here, value_lanes]
            scores = dot(keys, queries[h], 0, 0)
            weights = jnp.exp(jnp.where(mask, scores - totals[h], masked_value))
            slopes = dot(values, incoming[h], 0, 0)
            grad_scores = (weights * (slopes - row_dots[h])).astype(jnp.bfloat16)
            total_ref[block, here, value_lanes] += dot(
                incoming[h], weights.astype(jnp.bfloat16), 1, 1
            )
            total_ref[block, here, key_lanes] += dot(queries[h], grad_scores, 1, 1)
            result.append(carry[h] + dot(keys, grad_scores, 1, 0))
        return tuple(result)

    start = tuple(jnp.zeros((size, TILE), jnp.float32) for _ in range(heads))
    done = lax.fori_loop(0, high - low_ref[step] + 1, work, start)
    for h in range(heads):
        out_ref[step, places[h], rows:] = (done[h] * scale).astype(out_ref.dtype)

    @pl.when(step == pl.num_programs(0) - 1)
    def _():
        for block in range(out_ref.shape[0]):
            out_ref[block, :, :rows] = total_ref[block].astype(out_ref.dtype)


def attend_back(low, high, first, last, pack, slope, mixed, lse, heads, size, *behind):
    blocks, rows, lanes = pack.shape
    row_spec = pl.BlockSpec((1, 1, TILE), lambda i, *_: (i, 0, 0))
    whole = pl.BlockSpec((blocks, rows, lanes), lambda i, *_: (0, 0, 0))
    tile_spec = pl.BlockSpec((1, rows, TILE), lambda i, *_: (i, 0, 0))
    return pl.pallas_call(
        functools.partial(attend_back_kernel, heads, size),
        out_shape=jax.ShapeDtypeStruct(pack.shape, jnp.bfloat16),
        grid_spec=pltpu.PrefetchScalarGridSpec(
            num_scalar_prefetch=2,
            grid=(blocks,),
            in_specs=[
                row_spec,
                row_spec,
                whole,
                tile_spec,
                tile_spec,
                pl.BlockSpec((1, 8, TILE), lambda i, *_: (i, 0, 0)),
            ]
            + [pl.BlockSpec(memory_space=pl.ANY)] * len(behind),
            out_specs=whole,
            scratch_shapes=[pltpu.VMEM((blocks, rows, lanes - TILE), jnp.float32)],
        ),
        compiler_params=pltpu.CompilerParams(vmem_limit_bytes=40 * 1024 * 1024),
        cost_estimate=pl.CostEstimate(
            flops=10 * heads * size * TILE * TILE * 40,
            bytes_accessed=pack.size * 4,
            transcendentals=heads * TILE * TILE * 40,
        ),
        name="attend_back",
    )(low, high, first, last, pack, slope, mixed, lse, *behind)


def swap_with(value, bit):
    count = lax.axis_size(("rep", "shard"))
    return lax.ppermute(
        value, ("rep", "shard"), [(index, index ^ (1 << bit)) for index in range(count)]
    )


def bit_of(index, bit):
    return lax.rem(index // (1 << bit), 2)


class WeightSum:
    def __init__(self, grad, pieces=1, turned=False):
        count = lax.axis_size(("rep", "shard"))
        self.bits = count.bit_length() - 1
        self.shards = lax.axis_size("shard")
        self.shard_bits = self.shards.bit_length() - 1
        self.index = lax.axis_index("rep") * self.shards + lax.axis_index("shard")
        self.shape = grad.shape
        rows, columns = grad.shape
        names = list(range(self.shard_bits - 1, -1, -1))
        names += list(range(self.bits - 1, self.shard_bits - 1, -1))
        low = grad.astype(jnp.bfloat16)
        low = low.reshape((2,) * self.bits + (rows * columns // count // 768, pieces, 768 // pieces))
        self.parts = [low[..., piece, :] for piece in range(pieces)]
        self.left = [list(names) for _ in range(pieces)]
        self.orders = []
        for piece in range(pieces):
            order = list(range(self.bits))
            if (piece % 2 == 1) != turned:
                order[1:3] = order[2:0:-1]
            self.orders.append(order)

    def halve(self):
        for piece, part in enumerate(self.parts):
            bit = self.orders[piece].pop(0)
            axis = self.left[piece].index(bit)
            mine = bit_of(self.index, bit)
            keep = lax.dynamic_index_in_dim(part, mine, axis, keepdims=False)
            give = lax.dynamic_index_in_dim(part, 1 - mine, axis, keepdims=False)
            came = swap_with(give, bit)
            total = keep.astype(jnp.float32) + came.astype(jnp.float32)
            self.parts[piece] = total.astype(jnp.bfloat16)
            self.left[piece].remove(bit)
        return self.parts[0]

    def finish(self):
        while self.orders[0]:
            self.halve()
        for bit in range(self.bits - 1, self.shard_bits - 1, -1):
            mine = bit_of(self.index, bit)
            axis = self.bits - 1 - bit
            for piece, part in enumerate(self.parts):
                came = swap_with(part, bit)
                low = jnp.where(mine == 0, part, came)
                high = jnp.where(mine == 0, came, part)
                self.parts[piece] = jnp.stack([low, high], axis=axis)
        whole = jnp.stack(self.parts, axis=-2) if len(self.parts) > 1 else self.parts[0]
        return whole.reshape(self.shape[0] // self.shards, self.shape[1])


def reduce_small(value):
    for bit in range(lax.axis_size(("rep", "shard")).bit_length() - 1):
        value = value + swap_with(value, bit)
    return value


def body(
    tokens,
    cotangent,
    segment,
    w_qkv,
    bias_query,
    bias_value,
    w_out,
    bias_out,
    ln1_gain,
    ln1_bias,
    ln2_gain,
    ln2_bias,
    w_up,
    bias_up,
    w_down,
    bias_down,
):
    f32, bf16 = jnp.float32, jnp.bfloat16
    small = (
        bias_query, bias_value, bias_out, ln1_gain, ln1_bias, ln2_gain, ln2_bias, bias_down, bias_up,
    )
    sizes = [value.shape[0] for value in small]
    joined = lax.all_gather(jnp.concatenate(small), "shard", axis=0, tiled=False)
    full_small = []
    at = 0
    for length in sizes:
        full_small.append(joined[:, at : at + length].reshape(-1).astype(f32))
        at += length
    (
        query_bias, value_bias, out_bias, gain_one, offset_one, gain_two, offset_two, down_bias, up_bias,
    ) = full_small
    full_qkv = lax.all_gather(w_qkv, "shard", axis=0, tiled=True)
    full_wout = lax.all_gather(w_out, "shard", axis=0, tiled=True)
    full_wup = lax.all_gather(w_up, "shard", axis=0, tiled=True)
    full_wdown = lax.all_gather(w_down, "shard", axis=0, tiled=True)

    tok_rows, width = tokens.shape
    size = width // H
    shards = lax.axis_size("shard")
    heads = H // shards
    part = heads * size
    rep, shard = lax.axis_index("rep"), lax.axis_index("shard")
    halves = GROUP // shards
    side = lax.rem(rep, halves)
    parity = lax.rem(shard, 2)

    span = GROUP * tok_rows
    group_seg = lax.dynamic_slice_in_dim(segment, rep // halves * span, span, 0)
    one = jnp.sum((group_seg == group_seg[0]).astype(jnp.int32))
    two = span - jnp.sum((group_seg == group_seg[span - 1]).astype(jnp.int32))
    blocks = jnp.arange(GROUP, dtype=jnp.int32)
    high = 2 * blocks + jnp.where(blocks % 2 == 0, side, 1 - side)
    last = high[:, None] * TILE + jnp.arange(TILE, dtype=jnp.int32)[None, :]
    first = jnp.where(last >= two, two, jnp.where(last >= one, one, 0))
    low = first[:, 0] // TILE
    first, last = first[:, None, :], last[:, None, :]

    inputs = tokens.astype(f32)
    normed, norm_one_back = jax.vjp(layer_norm, inputs, gain_one, offset_one)
    normed_low = normed.astype(bf16)
    joined_bias = jnp.concatenate([query_bias, jnp.zeros_like(query_bias), value_bias])
    projected = (dot(full_qkv, normed_low, 0, 1) + joined_bias[:, None]).astype(bf16)
    parts = projected.reshape(3, shards, part, tok_rows)

    def by_side(value):
        near, far = value[..., :TILE], value[..., TILE:]
        swap = parity == 1
        return jnp.stack([jnp.where(swap, far, near), jnp.where(swap, near, far)], axis=0)

    def by_token(value):
        swap = parity == 1
        return jnp.concatenate(
            [jnp.where(swap, value[1], value[0]), jnp.where(swap, value[0], value[1])], axis=-1
        )

    pairs = jnp.concatenate([parts[1], parts[2]], axis=-1)
    message = jnp.concatenate(
        [jnp.broadcast_to(pairs[None], (halves,) + pairs.shape), by_side(parts[0])], axis=-1
    ).reshape(GROUP, part, 2 * tok_rows + TILE)
    pack = exchange(message, 1)
    mixed_tiles, lse = attend(low, high, first, last, pack, heads, size)
    back = exchange(mixed_tiles.astype(bf16), 2)
    mixed_low = by_token(back.reshape(halves, shards, part, TILE)).reshape(width, tok_rows)

    middle = inputs + dot(mixed_low, full_wout, 0, 0) + out_bias
    second, norm_two_back = jax.vjp(layer_norm, middle, gain_two, offset_two)
    second_low = second.astype(bf16)
    hidden = dot(second_low, full_wup, 1, 0) + up_bias
    active, gelu_back = jax.vjp(gelu_tanh, hidden)
    active_low = active.astype(bf16)
    layer_out = middle + dot(active_low, full_wdown, 1, 0) + down_bias
    grad_out = cotangent.astype(f32)
    sum_wdown = WeightSum(dot(active_low, cotangent, 0, 0))
    down_core = sum_wdown.halve()
    grad_down_bias = jnp.sum(grad_out, axis=0)
    (grad_hidden,) = gelu_back(dot(cotangent, full_wdown, 1, 1))
    hidden_low = grad_hidden.astype(bf16)
    sum_wup = WeightSum(dot(second_low, hidden_low, 0, 0), 1, True)
    up_start = sum_wup.parts[0]
    up_core = sum_wup.halve()
    grad_up_bias = jnp.sum(hidden_low.astype(f32), axis=0)
    grad_second = dot(hidden_low, full_wup, 1, 1)
    grad_middle_norm, grad_gain_two, grad_offset_two = norm_two_back(grad_second)
    grad_middle = grad_out + grad_middle_norm
    middle_low = grad_middle.astype(bf16)
    sum_wout = WeightSum(dot(mixed_low, middle_low, 1, 0))
    out_core = sum_wout.halve()
    grad_out_bias = jnp.sum(middle_low.astype(f32), axis=0)
    grad_mixed = dot(full_wout, middle_low, 1, 1).astype(bf16)

    slope = exchange(
        by_side(grad_mixed.reshape(shards, part, tok_rows)).reshape(GROUP, part, TILE), 3,
        down_core, up_start,
    )
    grad_pack = attend_back(low, high, first, last, pack, slope, mixed_tiles, lse, heads, size, up_core, out_core)
    returned = exchange(
        grad_pack, 4, sum_wdown.halve(), sum_wup.halve(), sum_wout.halve()
    ).reshape(halves, shards, part, 2 * tok_rows + TILE)
    grad_pairs = jnp.sum(returned[..., : 2 * tok_rows].astype(f32), axis=0).astype(bf16)
    grad_projected = jnp.stack(
        [
            by_token(returned[..., 2 * tok_rows :]),
            grad_pairs[..., :tok_rows],
            grad_pairs[..., tok_rows:],
        ],
        axis=0,
    ).reshape(3 * width, tok_rows)
    grad_wqkv = WeightSum(dot(normed_low, grad_projected, 0, 1), 2).finish()
    grad_wdown, grad_wup, grad_wout = sum_wdown.finish(), sum_wup.finish(), sum_wout.finish()
    bias_grads = jnp.sum(grad_projected.astype(f32), axis=1)
    grad_query_bias = bias_grads[:width]
    grad_value_bias = bias_grads[2 * width :]
    grad_normed = dot(grad_projected, full_qkv, 0, 1)
    grad_input_norm, grad_gain_one, grad_offset_one = norm_one_back(grad_normed)
    grad_input = grad_middle + grad_input_norm

    small_grads = (
        grad_query_bias, grad_value_bias, grad_out_bias, grad_gain_one, grad_offset_one,
        grad_gain_two, grad_offset_two, grad_down_bias, grad_up_bias,
    )
    laid = jnp.concatenate([value.reshape(shards, -1) for value in small_grads], axis=1)
    summed = lax.dynamic_index_in_dim(
        reduce_small(laid), shard, 0, keepdims=False
    )
    pieces = []
    at = 0
    for length in sizes:
        pieces.append(summed[at : at + length])
        at += length
    (
        sum_query_bias, sum_value_bias, sum_out_bias, sum_gain_one, sum_offset_one, sum_gain_two,
        sum_offset_two, sum_down_bias, sum_up_bias,
    ) = pieces
    return (
        layer_out,
        grad_input,
        grad_wqkv.astype(f32),
        sum_query_bias,
        sum_value_bias,
        grad_wout.astype(f32),
        sum_out_bias,
        sum_gain_one,
        sum_offset_one,
        sum_gain_two,
        sum_offset_two,
        grad_wup.astype(f32),
        sum_up_bias,
        grad_wdown.astype(f32),
        sum_down_bias,
    )


def solution(mesh):
    tokens_at, rows_at, vector_at = P(("rep", "shard"), None), P("shard", None), P("shard")
    return jax.shard_map(
        body,
        mesh=mesh,
        in_specs=(
            tokens_at, tokens_at, P(), rows_at, vector_at, vector_at, rows_at, vector_at, vector_at,
            vector_at, vector_at, vector_at, rows_at, vector_at, rows_at, vector_at,
        ),
        out_specs=(
            tokens_at, tokens_at, rows_at, vector_at, vector_at, rows_at, vector_at, vector_at,
            vector_at, vector_at, vector_at, rows_at, vector_at, rows_at, vector_at,
        ),
        check_vma=False,
    )
```
